256 devices in a mesh: row: 16 (over x_hi, z), col: 16 (over y, x_lo, core).
Axes of the slice: x: 4 (x_hi: 2, x_lo: 2; x = x_hi * 2 + x_lo), y: 4, z: 8, core: 2. Of those that a mesh axis runs over, the one named last changes fastest.
Arguments:
- start_block: bfloat16 [256, 16384], P('row', 'col'), may hold values from -6 to 6
- stiffness: bfloat16 [16, 16, 64, 128, 128], P('row', 'col'), as said below
- mass: bfloat16 [16, 16, 64, 128, 128], P('row', 'col'), as said below
- block_coords: int32 [16, 16, 64, 2], P('row', 'col'), may hold values from -1 to 7, as said below
- lower_bound: float32 [1], replicated, may hold values from 0 to 0.4
- upper_bound: float32 [1], replicated, may hold values from 1.6 to 2.4
Outputs:
- filtered: float32 [256, 16384], P('col', 'row')
The draws below stay inside these ranges and needn't reach their ends.
Inputs may be any that keep to these rules, and one draw needn't show every extreme that they name: `block_coords`: slot s of tile (r, c) names a block row and block column within the tile, or (-1, -1) when it is empty; live slots come before empty ones and no block is named twice. The pattern is symmetric: block (I, J) is live exactly when block (J, I) is, and every diagonal block is live. `stiffness`: K is symmetric: the slot of block (J, I) holds the transpose of the slot of block (I, J), and diagonal blocks are symmetric. `mass`: M is symmetric in the same way as K, on the same pattern.
All inputs are finite; a program needn't handle non-finite values.
Results may differ from the reference program's by a relative error of at most 0.0033.
Values may be sent and summed in bfloat16 or wider, within the bound.
A program may use at most 64 MiB of HBM per device.

```python
import jax
import jax.numpy as jnp
from jax import lax

NV = 256
BLK = 128
BR = 8
NB = 128
BC = 8
SLOTS = 64
DOFS = 16384
N_ROW = 16
N_COL = 16


def live_table(key):
    draws = jax.random.randint(jax.random.fold_in(key, 11), (NB, NB), 0, 8)
    rowpos = jnp.arange(NB)[:, None]
    colpos = jnp.arange(NB)[None, :]
    paired = jnp.where(rowpos <= colpos, draws, draws.T)
    near = jnp.abs(rowpos - colpos) < max(NB // 8, 2)
    return (rowpos == colpos) | (paired < jnp.where(near, 6, 2))


def slot_table(key):
    live = live_table(key)
    tiles = live.reshape(N_ROW, BR, N_COL, BC).transpose(0, 2, 1, 3).reshape(N_ROW, N_COL, SLOTS)
    order = jnp.argsort(1 - tiles.astype(jnp.int32), axis=-1, stable=True)
    alive = jnp.take_along_axis(tiles, order, axis=-1)
    return (order // BC, order % BC, alive)


def draw_block_coords(key, part):
    rows, cols, alive = slot_table(key)
    return jnp.stack([jnp.where(alive, rows, -1), jnp.where(alive, cols, -1)], axis=-1).astype(jnp.int32)


def block_values(key, salt, off_scale):
    rows, cols, alive = slot_table(key)
    glob_rows = jnp.arange(N_ROW)[:, None, None] * BR + rows
    glob_cols = jnp.arange(N_COL)[None, :, None] * BC + cols
    lower = jnp.minimum(glob_rows, glob_cols)
    upper = jnp.maximum(glob_rows, glob_cols)
    pairid = (lower * NB + upper).reshape(-1)
    flipped = (glob_rows > glob_cols).reshape(-1)
    onaxis = (glob_rows == glob_cols).reshape(-1)
    base = jax.random.fold_in(key, salt)
    ident = jnp.eye(BLK, dtype=jnp.float32)

    def one_block(items):
        pid, flip, same = items
        subkey = jax.random.fold_in(base, pid)
        raw = jax.random.normal(subkey, (BLK, BLK), jnp.float32)
        diagvals = jax.random.uniform(jax.random.fold_in(subkey, 7), (BLK,), jnp.float32, 0.5, 1.5)
        raw = raw * off_scale
        sym = 0.5 * (raw + raw.T) * (1.0 - ident) + diagvals[None, :] * ident
        return jnp.where(same, sym, jnp.where(flip, raw.T, raw))
    values = lax.map(one_block, (pairid, flipped, onaxis))
    return values.reshape(N_ROW, N_COL, SLOTS, BLK, BLK)


def draw_stiffness(key, part):
    return block_values(key, 21, 0.7 * (0.375 * NB * BLK) ** (-0.5)).astype(jnp.bfloat16)


def draw_mass(key, part):
    return block_values(key, 22, 0.4 * (0.375 * NB * BLK) ** (-0.5)).astype(jnp.bfloat16)


def block_scale(key, shape, cuts, smallest, high):
    factor_of = 1.0
    for dim, blocks in cuts:
        steps = jax.random.uniform(jax.random.fold_in(jax.random.fold_in(key, 6), dim), (blocks,), jnp.float32, smallest / len(cuts), high / len(cuts))
        factor_of = factor_of * jnp.repeat(jnp.exp(steps), shape[dim] // blocks).reshape((-1,) + (1,) * (len(shape) - 1 - dim))
    return factor_of


def gaussian(key, dims, scale, limit, shards=(), kind=jnp.bfloat16):
    result = jax.random.normal(key, dims, jnp.float32) * scale
    if len(shards) > 0:
        result = block_scale(key, dims, shards, -0.22, 0.18) * result
    return jnp.clip(result, min=-limit, max=limit).astype(kind)


def setup_inputs(seed: int = 0) -> dict:
    key_list = jax.random.split(jax.random.key(seed), 7)
    return {
        "start_block": gaussian(key_list[0], (NV, DOFS), 1.0, 6.0, ((0, 16), (1, 16))),
        "stiffness": draw_stiffness(jax.random.fold_in(key_list[6], 71), 0),
        "mass": draw_mass(jax.random.fold_in(key_list[6], 71), 0),
        "block_coords": draw_block_coords(jax.random.fold_in(key_list[6], 71), 0),
        "lower_bound": jnp.clip(jax.random.uniform(key_list[4], (1,), jnp.float32, 0.0, 0.4), 0.0, 0.4),
        "upper_bound": jnp.clip(jax.random.uniform(key_list[5], (1,), jnp.float32, 1.6, 2.4), 1.6, 2.4),
    }


def tile_apply(vecs, kvals, mvals, coords, centre, scale):
    width = vecs.shape[0]
    nsource = vecs.shape[1] // BLK
    blocks = vecs.astype(jnp.float32).reshape(width, nsource, BLK)
    picks = jnp.clip(coords[:, 1], 0, nsource - 1).astype(jnp.int32)
    picked = jnp.take(blocks, picks, axis=1)
    kpart = jnp.einsum("psj,sij->psi", picked, kvals.astype(jnp.float32), precision=lax.Precision.HIGHEST)
    mpart = jnp.einsum("psj,sij->psi", picked, mvals.astype(jnp.float32), precision=lax.Precision.HIGHEST)
    terms = (kpart - centre * mpart) * scale
    placing = (coords[:, 0][:, None] == jnp.arange(BR, dtype=jnp.int32)[None, :]).astype(jnp.float32)
    placed = jnp.einsum("psi,sb->pbi", terms, placing, precision=lax.Precision.HIGHEST)
    return placed.reshape(width, BR * BLK)


def apply_pencil(vecs, stiffness, mass, block_coords, centre, scale):
    segments = vecs.reshape(NV, N_COL, BC * BLK)

    def row_part(rowidx):
        def add_tile(total, colidx):
            part = tile_apply(segments[:, colidx], stiffness[rowidx, colidx], mass[rowidx, colidx], block_coords[rowidx, colidx], centre, scale)
            return total + part, None

        total, _ = lax.scan(add_tile, jnp.zeros((NV, BR * BLK), jnp.float32), jnp.arange(N_COL, dtype=jnp.int32))
        return total

    parts = lax.map(row_part, jnp.arange(N_ROW, dtype=jnp.int32))
    return jnp.transpose(parts, (1, 0, 2)).reshape(NV, DOFS)


def reference(start_block, stiffness, mass, block_coords, lower_bound, upper_bound):
    centre = 0.5 * (lower_bound[0] + upper_bound[0])
    half = 0.5 * (upper_bound[0] - lower_bound[0])
    first_scale = 1.0 / half
    next_scale = 2.0 / half
    first = apply_pencil(start_block, stiffness, mass, block_coords, centre, first_scale).astype(jnp.bfloat16)
    second = (apply_pencil(first, stiffness, mass, block_coords, centre, next_scale) - start_block.astype(jnp.float32)).astype(jnp.bfloat16)
    filtered = apply_pencil(second, stiffness, mass, block_coords, centre, next_scale) - first.astype(jnp.float32)
    return filtered
```

```python
import jax
import jax.numpy as jnp
from jax import lax
from jax.experimental import pallas as pl
from jax.experimental.pallas import tpu as pltpu
from jax.sharding import PartitionSpec as P

MESH = pl.DeviceIdType.MESH
BLK = 128
BR = 8
TILE = 1024
PIECE = 16
NS = 8
TOP = 32766.0
TINY = 1e-33
ROW_NEAR = (1, 7, 2, 6, 3, 5, 4)
ROW_FAR = (4, 3, 5, 2, 6, 1, 7)
COL_NEAR = (4, 1, 3, 5, 7, 2, 6)
COL_FAR = (6, 2, 5, 7, 1, 3, 4)


def back(axis, o):
    return (-o) % NS if axis == "row" else (o // 4) * 4 + (-o) % 4


def rem(a, b):
    return lax.rem(a, jnp.int32(b))


def div(a, b):
    return lax.div(a, jnp.int32(b))


def flip(bit, s):
    return 1 - bit if s else bit


def kernel(inv, lower, upper, start, khbm, mhbm, out, kslot, mslot, kd, md, ybuf, ag, qsib, rsib, qring, rring, own, keep,
           s_sib, s_ring, r_sib, r_ring, local_sem, send_sem, recv_sem, ssend_sem, srecv_sem):
    r = lax.axis_index("row")
    c = lax.axis_index("col")
    xh, z = div(r, NS), rem(r, NS)
    y, xl, core = div(c, 4), rem(div(c, 2), 2), rem(c, 2)

    def member(axis, s, o):
        if axis == "row":
            return flip(xh, s) * NS + rem(z + o, NS)
        return rem(y + o % 4, 4) * 4 + flip(xl, o // 4) * 2 + flip(core, s)

    def device(axis, s, o):
        m = member(axis, s, o)
        return (m, c) if axis == "row" else (r, m)

    kcopy = pltpu.make_async_copy(khbm, kslot, local_sem.at[0])
    mcopy = pltpu.make_async_copy(mhbm, mslot, local_sem.at[1])
    kcopy.start()
    mcopy.start()

    barrier = pltpu.get_barrier_semaphore()
    for axis in ("row", "col"):
        for o in range(1, NS):
            pl.semaphore_signal(barrier, inc=1, device_id=device(axis, 0, o), device_id_type=MESH)
        pl.semaphore_signal(barrier, inc=1, device_id=device(axis, 1, 0), device_id_type=MESH)

    centre = 0.5 * (lower[0] + upper[0])
    half = 0.5 * (upper[0] - lower[0])

    kcopy.wait()
    mcopy.wait()
    for t in range(BR * BR):
        s = inv[t]
        live = s >= 0
        s = jnp.maximum(s, 0)
        rows, cols = pl.ds((t // BR) * BLK, BLK), pl.ds((t % BR) * BLK, BLK)
        kd[rows, cols] = jnp.where(live, kslot[s], jnp.zeros((BLK, BLK), jnp.bfloat16))
        md[rows, cols] = jnp.where(live, mslot[s], jnp.zeros((BLK, BLK), jnp.bfloat16))

    pl.semaphore_wait(barrier, 2 * NS)

    sent = []

    def copy(n, side, src, dst, i, j, dev, sems=(send_sem, recv_sem)):
        return pltpu.make_async_remote_copy(
            src_ref=src, dst_ref=dst, send_sem=sems[0].at[n, side, i], recv_sem=sems[1].at[n, side, j],
            device_id=dev, device_id_type=MESH)

    def push(*args, **kw):
        one = copy(*args, **kw)
        one.start()
        sent.append(one)

    def arrived(n, side, dst, j, sems=(send_sem, recv_sem)):
        copy(n, side, dst, dst, 0, j, (r, c), sems).wait_recv()

    def gather(g, n, axis, src, order_out, order_in):
        buf = ag.at[g]
        push(n, 1, src, buf.at[NS], 0, 0, device(axis, 1, 0))
        for o in order_out:
            j = back(axis, o)
            push(n, 0, src, buf.at[j], o, j, device(axis, 0, o))
        buf[0] = src[...]
        for o in order_in:
            arrived(n, 0, buf.at[o], o)
            push(n, 1, buf.at[o], buf.at[NS + o], o, o, device(axis, 1, 0))
        for o in (0,) + order_in:
            arrived(n, 1, buf.at[NS + o], o)

    def quantize(part, q, sc):
        top = jnp.maximum(jnp.max(jnp.abs(part), keepdims=True), TINY)
        q[...] = jnp.round(part * (TOP / top)).astype(jnp.int32).astype(jnp.int16)
        sc[...] = jnp.broadcast_to(top * (1.0 / TOP), (1, BLK))

    def value(q, sc):
        return q[...].astype(jnp.int32).astype(jnp.float32) * sc[:, :1]

    scale_sems = (ssend_sem, srecv_sem)

    def scatter(m, n, axis, order):
        for o in order + (0,):
            quantize(ybuf[NS + o], qsib.at[m, o], s_sib.at[m, o])
            push(n, 1, qsib.at[m, o], rsib.at[m, o], o, o, device(axis, 1, 0))
            push(n, 1, s_sib.at[m, o], r_sib.at[m, o], o, o, device(axis, 1, 0), scale_sems)
        total = None
        for o in order + (0,):
            arrived(n, 1, rsib.at[m, o], o)
            arrived(n, 1, r_sib.at[m, o], o, scale_sems)
            part = ybuf[o] + value(rsib.at[m, o], r_sib.at[m, o])
            if o:
                j = back(axis, o)
                quantize(part, qring.at[m, o], s_ring.at[m, o])
                push(n, 0, qring.at[m, o], rring.at[m, j], o, j, device(axis, 0, o))
                push(n, 0, s_ring.at[m, o], r_ring.at[m, j], o, j, device(axis, 0, o), scale_sems)
            else:
                total = part
        own[...] = total
        for o in reversed(order):
            arrived(n, 0, rring.at[m, o], o)
            arrived(n, 0, r_ring.at[m, o], o, scale_sems)
            own[...] += value(rring.at[m, o], r_ring.at[m, o])
        return own[...]

    def product(g, come, go, scale, transposed):
        rows = []
        for s in (0, 1):
            for o in range(NS):
                v = member(go, s, o)
                if come == "row":
                    slot = rem(div(v, NS) + xh, 2) * NS + rem(rem(v, NS) - z + NS, NS)
                else:
                    slot = rem(v + core, 2) * NS + rem(div(v, 2) + xl, 2) * 4 + rem(div(v, 4) - y + 4, 4)
                rows.append(ag[g, slot])
        x = jnp.concatenate(rows, axis=0)
        dims = (((1,), (1,)), ((), ())) if transposed else (((1,), (0,)), ((), ()))
        kpart = lax.dot_general(x, kd[...], dims, preferred_element_type=jnp.float32)
        mpart = lax.dot_general(x, md[...], dims, preferred_element_type=jnp.float32)
        ybuf[...] = ((kpart - centre * mpart) * scale).reshape(2 * NS, PIECE, TILE)

    gather(0, 0, "row", start, ROW_NEAR, ROW_NEAR)
    product(0, "row", "col", 1.0 / half, True)
    keep[0] = scatter(0, 1, "col", COL_FAR).astype(jnp.bfloat16)
    gather(1, 2, "col", keep.at[0], COL_FAR, COL_NEAR)
    product(1, "col", "row", 2.0 / half, False)
    keep[1] = (scatter(1, 3, "row", ROW_FAR) - start[...].astype(jnp.float32)).astype(jnp.bfloat16)
    gather(2, 4, "row", keep.at[1], ROW_NEAR, ROW_NEAR)
    product(2, "row", "col", 2.0 / half, True)
    out[...] = scatter(2, 5, "col", COL_FAR) - keep[0].astype(jnp.float32)
    for one in sent:
        one.wait_send()


def local(start, stiffness, mass, coords, lower, upper):
    pairs = coords[0, 0]
    place = jnp.where(pairs[:, 0] < 0, -1, pairs[:, 0] * BR + pairs[:, 1])
    slots = place.shape[0]
    found = place[None, :] == jnp.arange(BR * BR, dtype=jnp.int32)[:, None]
    inv = jnp.max(jnp.where(found, jnp.arange(slots, dtype=jnp.int32)[None, :], -1), axis=1)
    smem, vmem, hbm = (pl.BlockSpec(memory_space=m) for m in (pltpu.SMEM, pltpu.VMEM, pl.ANY))
    half = (3, NS, PIECE, TILE)
    scales = pltpu.VMEM((3, NS, 1, BLK), jnp.float32)
    sems = pltpu.SemaphoreType.DMA((6, 2, NS))
    return pl.pallas_call(
        kernel,
        out_shape=jax.ShapeDtypeStruct(start.shape, jnp.float32),
        in_specs=[smem, smem, smem, vmem, hbm, hbm],
        out_specs=vmem,
        scratch_shapes=[
            pltpu.VMEM((slots, BLK, BLK), jnp.bfloat16),
            pltpu.VMEM((slots, BLK, BLK), jnp.bfloat16),
            pltpu.VMEM((TILE, TILE), jnp.bfloat16),
            pltpu.VMEM((TILE, TILE), jnp.bfloat16),
            pltpu.VMEM((2 * NS, PIECE, TILE), jnp.float32),
            pltpu.VMEM((3, 2 * NS, PIECE, TILE), jnp.bfloat16),
            pltpu.VMEM(half, jnp.int16),
            pltpu.VMEM(half, jnp.int16),
            pltpu.VMEM(half, jnp.int16),
            pltpu.VMEM(half, jnp.int16),
            pltpu.VMEM((PIECE, TILE), jnp.float32),
            pltpu.VMEM((2, PIECE, TILE), jnp.bfloat16),
            scales, scales, scales, scales,
            pltpu.SemaphoreType.DMA((2,)),
            sems, sems, sems, sems,
        ],
        compiler_params=pltpu.CompilerParams(
            collective_id=0, has_side_effects=True, vmem_limit_bytes=56 * 2**20
        ),
        name="filter",
    )(inv, lower, upper, start, stiffness.reshape(stiffness.shape[2:]), mass.reshape(mass.shape[2:]))


def solution(mesh):
    placed = (
        P("row", "col"),
        P("row", "col", None, None, None),
        P("row", "col", None, None, None),
        P("row", "col", None, None),
        P(),
        P(),
    )
    return jax.shard_map(
        local, mesh=mesh, in_specs=placed, out_specs=P("col", "row"), check_vma=False
    )
```

```python
import jax
import jax.numpy as jnp
from jax import lax
from jax.experimental import pallas as pl
from jax.experimental.pallas import tpu as pltpu
from jax.sharding import PartitionSpec as P

MESH = pl.DeviceIdType.MESH
BLK = 128
BR = 8
TILE = 1024
PIECE = 16
G = 2
ROWS = PIECE // G
WIDE = TILE // G
ORDER = (
    (0, 0), (1, 0), (0, 1), (1, 1), (0, 2), (0, 3), (1, 2), (1, 3), (0, 4), (1, 4), (0, 5), (0, 6), (1, 5),
    (1, 6), (0, 7), (1, 7), (0, 8), (1, 8), (0, 9), (1, 9), (0, 10), (0, 11), (1, 10), (1, 11), (0, 12), (1, 12),
)
NS = 8
TOP = 32766.0
TINY = 1e-33
ROW_NEAR = (1, 7, 2, 6, 3, 5, 4)
ROW_FAR = (4, 3, 5, 2, 6, 1, 7)
COL_NEAR = (4, 1, 3, 5, 7, 2, 6)
COL_FAR = (6, 2, 5, 7, 1, 3, 4)


def back(axis, o):
    return (-o) % NS if axis == "row" else (o // 4) * 4 + (-o) % 4


def rem(a, b):
    return lax.rem(a, jnp.int32(b))


def div(a, b):
    return lax.div(a, jnp.int32(b))


def flip(bit, s):
    return 1 - bit if s else bit


def kernel(pairs, lower, upper, start_hbm, khbm, mhbm, out, first_out, start, place, limits, inv_wide, inv, kslot, mslot, kt, mt, kd, md, ybuf, ag, qsib, rsib, qring, rring, own, keep,
           s_sib, s_ring, r_sib, r_ring, local_sem, send_sem, recv_sem, ssend_sem, srecv_sem):
    r = lax.axis_index("row")
    c = lax.axis_index("col")
    xh, z = div(r, NS), rem(r, NS)
    y, xl, core = div(c, 4), rem(div(c, 2), 2), rem(c, 2)

    def member(axis, s, o):
        if axis == "row":
            return flip(xh, s) * NS + rem(z + o, NS)
        return rem(y + o % 4, 4) * 4 + flip(xl, o // 4) * 2 + flip(core, s)

    def device(axis, s, o):
        m = member(axis, s, o)
        return (m, c) if axis == "row" else (r, m)

    barrier = pltpu.get_barrier_semaphore()
    for axis in ("row", "col"):
        for o in range(1, NS):
            pl.semaphore_signal(barrier, inc=1, device_id=device(axis, 0, o), device_id_type=MESH)
        pl.semaphore_signal(barrier, inc=1, device_id=device(axis, 1, 0), device_id_type=MESH)

    loads = [
        pltpu.make_async_copy(src, dst, local_sem.at[i])
        for i, (src, dst) in enumerate(
            ((start_hbm, start), (pairs, place), (khbm, kslot), (mhbm, mslot),
             (lower, limits.at[0]), (upper, limits.at[1]))
        )
    ]
    for load in loads:
        load.start()

    def pack(part):
        return part if G == 1 else jnp.concatenate([part[:, :WIDE], part[:, WIDE:]], axis=0)

    def unpack(piece):
        return piece if G == 1 else jnp.concatenate([piece[:ROWS], piece[ROWS:]], axis=1)

    loads[0].wait()
    for g in range(G):
        keep[2, g] = pack(start[...].astype(jnp.float32)[g * ROWS:(g + 1) * ROWS]).astype(jnp.bfloat16)

    def build():
        slots = place.shape[1]
        target = lax.broadcasted_iota(jnp.int32, (BR * BR, slots), 0)
        slot = lax.broadcasted_iota(jnp.int32, (BR * BR, slots), 1)
        found = (place[0:1] == target // BR) & (place[1:2] == target % BR)
        held_by = jnp.max(jnp.where(found, slot, -1), axis=1, keepdims=True)
        inv_wide[...] = jnp.broadcast_to(held_by, inv_wide.shape)
        index = pltpu.make_async_copy(inv_wide, inv, local_sem.at[6])
        index.start()
        index.wait()
        loads[2].wait()
        loads[3].wait()
        for t in range(BR * BR):
            s = inv[t, 0]
            live = s >= 0
            s = jnp.maximum(s, 0)
            zero = jnp.zeros((BLK, BLK), jnp.bfloat16)
            rows, cols = slice((t // BR) * BLK, (t // BR + 1) * BLK), slice((t % BR) * BLK, (t % BR + 1) * BLK)
            kblock = jnp.where(live, kslot[s], zero)
            mblock = jnp.where(live, mslot[s], zero)
            kd[rows, cols] = kblock
            md[rows, cols] = mblock
            kt[cols, rows] = kblock.T
            mt[cols, rows] = mblock.T

    pl.semaphore_wait(barrier, 2 * NS)

    sent = []

    def copy(g, n, side, src, dst, i, j, dev, sems=(send_sem, recv_sem)):
        return pltpu.make_async_remote_copy(
            src_ref=src, dst_ref=dst, send_sem=sems[0].at[g, n, side, i], recv_sem=sems[1].at[g, n, side, j],
            device_id=dev, device_id_type=MESH)

    def push(*args, **kw):
        one = copy(*args, **kw)
        one.start()
        sent.append(one)

    def arrived(g, n, side, dst, j, sems=(send_sem, recv_sem)):
        copy(g, n, side, dst, dst, 0, j, (r, c), sems).wait_recv()

    def near(axis):
        return ROW_NEAR if axis == "row" else COL_NEAR

    def far(axis):
        return ROW_FAR if axis == "row" else COL_FAR

    def gather_send(g, m, n, axis, src):
        buf = ag.at[m, g]
        push(g, n, 1, src, buf.at[NS], 0, 0, device(axis, 1, 0))
        for o in ROW_NEAR if axis == "row" else COL_FAR:
            j = back(axis, o)
            push(g, n, 0, src, buf.at[j], o, j, device(axis, 0, o))
        buf[0] = src[...]

    def gather_pass(g, m, n, axis):
        buf = ag.at[m, g]
        for o in near(axis):
            arrived(g, n, 0, buf.at[o], o)
            push(g, n, 1, buf.at[o], buf.at[NS + o], o, o, device(axis, 1, 0))

    def gather_end(g, m, n, axis):
        for o in (0,) + near(axis):
            arrived(g, n, 1, ag.at[m, g, NS + o], o)

    def quantize(part, q, sc):
        top = jnp.maximum(jnp.max(jnp.abs(part), keepdims=True), TINY)
        q[...] = jnp.round(pack(part * (TOP / top))).astype(jnp.int32).astype(jnp.int16)
        sc[...] = jnp.broadcast_to(top * (1.0 / TOP), (1, BLK))

    def value(q, sc):
        return unpack(q[...].astype(jnp.int32).astype(jnp.float32)) * sc[:, :1]

    scale_sems = (ssend_sem, srecv_sem)

    def scatter_send(g, m, n, axis):
        for o in far(axis) + (0,):
            quantize(ybuf[g, NS + o], qsib.at[m, g, o], s_sib.at[m, g, o])
            push(g, n, 1, qsib.at[m, g, o], rsib.at[m, g, o], o, o, device(axis, 1, 0))
            push(g, n, 1, s_sib.at[m, g, o], r_sib.at[m, g, o], o, o, device(axis, 1, 0), scale_sems)

    def scatter_pass(g, m, n, axis):
        for o in far(axis) + (0,):
            arrived(g, n, 1, rsib.at[m, g, o], o)
            arrived(g, n, 1, r_sib.at[m, g, o], o, scale_sems)
            part = ybuf[g, o] + value(rsib.at[m, g, o], r_sib.at[m, g, o])
            if o:
                j = back(axis, o)
                quantize(part, qring.at[m, g, o], s_ring.at[m, g, o])
                push(g, n, 0, qring.at[m, g, o], rring.at[m, g, j], o, j, device(axis, 0, o))
                push(g, n, 0, s_ring.at[m, g, o], r_ring.at[m, g, j], o, j, device(axis, 0, o), scale_sems)
            else:
                own[g] = part

    def scatter_end(g, m, n, axis):
        total = own[g]
        for o in near(axis):
            arrived(g, n, 0, rring.at[m, g, o], o)
            arrived(g, n, 0, r_ring.at[m, g, o], o, scale_sems)
            total = total + value(rring.at[m, g, o], r_ring.at[m, g, o])
        return total

    def product(g, m, come, go, scale, transposed):
        low, high = limits[0], limits[1]
        centre, half = 0.5 * (low + high), 0.5 * (high - low)
        rows = []
        for s in (0, 1):
            for o in range(NS):
                v = member(go, s, o)
                if come == "row":
                    slot = rem(div(v, NS) + xh, 2) * NS + rem(rem(v, NS) - z + NS, NS)
                else:
                    slot = rem(v + core, 2) * NS + rem(div(v, 2) + xl, 2) * 4 + rem(div(v, 4) - y + 4, 4)
                rows.append(unpack(ag[m, g, slot].astype(jnp.float32)) if G > 1 else ag[m, g, slot])
        x = jnp.concatenate(rows, axis=0).astype(jnp.bfloat16)
        kpart = jnp.dot(x, (kt if transposed else kd)[...], preferred_element_type=jnp.float32)
        mpart = jnp.dot(x, (mt if transposed else md)[...], preferred_element_type=jnp.float32)
        ybuf[g] = ((kpart - centre * mpart) * (scale / half)).reshape(2 * NS, ROWS, TILE)

    def held(m, g):
        return unpack(keep[m, g].astype(jnp.float32))

    def step(g, t):
        rows = slice(g * ROWS, (g + 1) * ROWS)
        if t == 0:
            gather_send(g, 0, 0, "row", keep.at[2, g])
        elif t == 1:
            gather_pass(g, 0, 0, "row")
        elif t == 2:
            gather_end(g, 0, 0, "row")
            product(g, 0, "row", "col", 1.0, True)
            scatter_send(g, 0, 1, "col")
        elif t == 3:
            scatter_pass(g, 0, 1, "col")
        elif t == 4:
            keep[0, g] = pack(scatter_end(g, 0, 1, "col")).astype(jnp.bfloat16)
            gather_send(g, 1, 2, "col", keep.at[0, g])
        elif t == 5:
            gather_pass(g, 1, 2, "col")
        elif t == 6:
            gather_end(g, 1, 2, "col")
            product(g, 1, "col", "row", 2.0, False)
            scatter_send(g, 1, 3, "row")
        elif t == 7:
            scatter_pass(g, 1, 3, "row")
        elif t == 8:
            keep[1, g] = pack(scatter_end(g, 1, 3, "row") - held(2, g)).astype(jnp.bfloat16)
            gather_send(g, 2, 4, "row", keep.at[1, g])
        elif t == 9:
            gather_pass(g, 2, 4, "row")
        elif t == 10:
            gather_end(g, 2, 4, "row")
            product(g, 2, "row", "col", 2.0, True)
            scatter_send(g, 2, 5, "col")
        elif t == 11:
            scatter_pass(g, 2, 5, "col")
        else:
            out[rows] = scatter_end(g, 2, 5, "col")
            first_out[rows] = held(0, g)

    for n, (g, t) in enumerate(ORDER):
        if n == G:
            for load in (loads[1], loads[4], loads[5]):
                load.wait()
            build()
        step(g, t)
    for one in sent:
        one.wait_send()


def local(start, stiffness, mass, coords, lower, upper):
    slots = stiffness.shape[2]
    vmem, hbm = (pl.BlockSpec(memory_space=m) for m in (pltpu.VMEM, pl.ANY))
    half = (3, G, NS, PIECE, WIDE)
    scales = pltpu.VMEM((3, G, NS, 1, BLK), jnp.float32)
    sems = pltpu.SemaphoreType.DMA((G, 6, 2, NS))
    total, first = pl.pallas_call(
        kernel,
        out_shape=[jax.ShapeDtypeStruct(start.shape, jnp.float32)] * 2,
        in_specs=[hbm] * 6,
        out_specs=[vmem] * 2,
        scratch_shapes=[
            pltpu.VMEM(start.shape, start.dtype),
            pltpu.VMEM((2, slots), jnp.int32),
            pltpu.VMEM((2, 1, 1), jnp.float32),
            pltpu.VMEM((BR * BR, BLK), jnp.int32),
            pltpu.SMEM((BR * BR, BLK), jnp.int32),
            pltpu.VMEM((slots, BLK, BLK), jnp.bfloat16),
            pltpu.VMEM((slots, BLK, BLK), jnp.bfloat16),
            pltpu.VMEM((TILE, TILE), jnp.bfloat16),
            pltpu.VMEM((TILE, TILE), jnp.bfloat16),
            pltpu.VMEM((TILE, TILE), jnp.bfloat16),
            pltpu.VMEM((TILE, TILE), jnp.bfloat16),
            pltpu.VMEM((G, 2 * NS, ROWS, TILE), jnp.float32),
            pltpu.VMEM((3, G, 2 * NS, PIECE, WIDE), jnp.bfloat16),
            pltpu.VMEM(half, jnp.int16),
            pltpu.VMEM(half, jnp.int16),
            pltpu.VMEM(half, jnp.int16),
            pltpu.VMEM(half, jnp.int16),
            pltpu.VMEM((G, ROWS, TILE), jnp.float32),
            pltpu.VMEM((3, G, PIECE, WIDE), jnp.bfloat16),
            scales, scales, scales, scales,
            pltpu.SemaphoreType.DMA((7,)),
            sems, sems, sems, sems,
        ],
        compiler_params=pltpu.CompilerParams(
            collective_id=0, has_side_effects=True, vmem_limit_bytes=56 * 2**20
        ),
        name="filter",
    )(coords[0, 0].T, lower.reshape(1, 1), upper.reshape(1, 1), start,
      stiffness.reshape(stiffness.shape[2:]), mass.reshape(mass.shape[2:]))
    return total - first


def solution(mesh):
    placed = (
        P("row", "col"),
        P("row", "col", None, None, None),
        P("row", "col", None, None, None),
        P("row", "col", None, None),
        P(),
        P(),
    )
    return jax.shard_map(
        local, mesh=mesh, in_specs=placed, out_specs=P("col", "row"), check_vma=False
    )
```

```python
import jax
import jax.numpy as jnp
from jax import lax
from jax.experimental import pallas as pl
from jax.experimental.pallas import tpu as pltpu
from jax.sharding import PartitionSpec as P

MESH = pl.DeviceIdType.MESH
BLK = 128
BR = 8
TILE = 1024
PIECE = 16
G = 2
ROWS = PIECE // G
WIDE = TILE // G
ORDER = (
    (0, 0), (1, 0), (0, 1), (1, 1), (0, 2), (0, 3), (1, 2), (1, 3), (0, 4), (1, 4), (0, 5), (0, 6), (1, 5),
    (1, 6), (0, 7), (1, 7), (0, 8), (1, 8), (0, 9), (1, 9), (0, 10), (0, 11), (1, 10), (1, 11), (0, 12), (1, 12),
)
NS = 8
TOP = 32766.0
TINY = 1e-33
ROW_NEAR = (1, 7, 2, 6, 3, 5, 4)
ROW_FAR = (4, 3, 5, 2, 6, 1, 7)
COL_NEAR = (4, 1, 3, 5, 7, 2, 6)
COL_FAR = (6, 2, 5, 7, 1, 3, 4)


def back(axis, o):
    return (-o) % NS if axis == "row" else (o // 4) * 4 + (-o) % 4


def rem(a, b):
    return lax.rem(a, jnp.int32(b))


def div(a, b):
    return lax.div(a, jnp.int32(b))


def flip(bit, s):
    return 1 - bit if s else bit


def kernel(pairs, lower, upper, start_hbm, khbm, mhbm, out, first_out, start, place, limits, inv_wide, inv, kslot, mslot, kt, mt, kd, md, ybuf, ag, qsib, rsib, qring, rring, own, keep,
           s_sib, s_ring, r_sib, r_ring, local_sem, send_sem, recv_sem, ssend_sem, srecv_sem):
    r = lax.axis_index("row")
    c = lax.axis_index("col")
    xh, z = div(r, NS), rem(r, NS)
    y, xl, core = div(c, 4), rem(div(c, 2), 2), rem(c, 2)

    def member(axis, s, o):
        if axis == "row":
            return flip(xh, s) * NS + rem(z + o, NS)
        return rem(y + o % 4, 4) * 4 + flip(xl, o // 4) * 2 + flip(core, s)

    def device(axis, s, o):
        m = member(axis, s, o)
        return (m, c) if axis == "row" else (r, m)

    barrier = pltpu.get_barrier_semaphore()
    for axis in ("row", "col"):
        for o in range(1, NS):
            pl.semaphore_signal(barrier, inc=1, device_id=device(axis, 0, o), device_id_type=MESH)
        pl.semaphore_signal(barrier, inc=1, device_id=device(axis, 1, 0), device_id_type=MESH)

    loads = [
        pltpu.make_async_copy(src, dst, local_sem.at[i])
        for i, (src, dst) in enumerate(
            ((start_hbm, start), (pairs, place), (khbm, kslot), (mhbm, mslot),
             (lower, limits.at[0]), (upper, limits.at[1]))
        )
    ]
    for load in loads:
        load.start()

    def pack(part):
        return part if G == 1 else jnp.concatenate([part[:, :WIDE], part[:, WIDE:]], axis=0)

    def unpack(piece):
        return piece if G == 1 else jnp.concatenate([piece[:ROWS], piece[ROWS:]], axis=1)

    loads[0].wait()
    for g in range(G):
        keep[2, g] = pack(start[...].astype(jnp.float32)[g * ROWS:(g + 1) * ROWS]).astype(jnp.bfloat16)

    def build():
        slots = place.shape[1]
        target = lax.broadcasted_iota(jnp.int32, (BR * BR, slots), 0)
        slot = lax.broadcasted_iota(jnp.int32, (BR * BR, slots), 1)
        found = (place[0:1] == target // BR) & (place[1:2] == target % BR)
        held_by = jnp.max(jnp.where(found, slot, -1), axis=1, keepdims=True)
        inv_wide[...] = jnp.broadcast_to(held_by, inv_wide.shape)
        index = pltpu.make_async_copy(inv_wide, inv, local_sem.at[6])
        index.start()
        index.wait()
        loads[2].wait()
        loads[3].wait()
        for t in range(BR * BR):
            s = inv[t, 0]
            live = s >= 0
            s = jnp.maximum(s, 0)
            zero = jnp.zeros((BLK, BLK), jnp.bfloat16)
            rows, cols = slice((t // BR) * BLK, (t // BR + 1) * BLK), slice((t % BR) * BLK, (t % BR + 1) * BLK)
            kblock = jnp.where(live, kslot[s], zero)
            mblock = jnp.where(live, mslot[s], zero)
            kd[rows, cols] = kblock
            md[rows, cols] = mblock
            kt[cols, rows] = kblock.T
            mt[cols, rows] = mblock.T

    pl.semaphore_wait(barrier, 2 * NS)

    sent = []

    def copy(g, n, side, src, dst, i, j, dev, sems=(send_sem, recv_sem)):
        return pltpu.make_async_remote_copy(
            src_ref=src, dst_ref=dst, send_sem=sems[0].at[g, n, side, i], recv_sem=sems[1].at[g, n, side, j],
            device_id=dev, device_id_type=MESH)

    def push(*args, **kw):
        one = copy(*args, **kw)
        one.start()
        sent.append(one)

    def arrived(g, n, side, dst, j, sems=(send_sem, recv_sem)):
        copy(g, n, side, dst, dst, 0, j, (r, c), sems).wait_recv()

    def near(axis):
        return ROW_NEAR if axis == "row" else COL_NEAR

    def far(axis):
        return ROW_FAR if axis == "row" else COL_FAR

    def gather_send(g, m, n, axis, src):
        buf = ag.at[m, g]
        push(g, n, 1, src, buf.at[NS], 0, 0, device(axis, 1, 0))
        for o in ROW_NEAR if axis == "row" else COL_FAR:
            j = back(axis, o)
            push(g, n, 0, src, buf.at[j], o, j, device(axis, 0, o))
        buf[0] = src[...]

    def gather_pass(g, m, n, axis):
        buf = ag.at[m, g]
        for o in near(axis):
            arrived(g, n, 0, buf.at[o], o)
            push(g, n, 1, buf.at[o], buf.at[NS + o], o, o, device(axis, 1, 0))

    def gather_end(g, m, n, axis):
        for o in (0,) + near(axis):
            arrived(g, n, 1, ag.at[m, g, NS + o], o)

    def quantize(part, q, sc):
        top = jnp.maximum(jnp.max(jnp.abs(part), keepdims=True), TINY)
        q[...] = jnp.round(pack(part * (TOP / top))).astype(jnp.int32).astype(jnp.int16)
        sc[...] = jnp.broadcast_to(top * (1.0 / TOP), (1, BLK))

    def value(q, sc):
        return unpack(q[...].astype(jnp.int32).astype(jnp.float32)) * sc[:, :1]

    scale_sems = (ssend_sem, srecv_sem)

    def scatter_send(g, m, n, axis):
        for o in far(axis) + (0,):
            quantize(ybuf[g, NS + o], qsib.at[m, g, o], s_sib.at[m, g, o])
            push(g, n, 1, qsib.at[m, g, o], rsib.at[m, g, o], o, o, device(axis, 1, 0))
            push(g, n, 1, s_sib.at[m, g, o], r_sib.at[m, g, o], o, o, device(axis, 1, 0), scale_sems)

    def scatter_pass(g, m, n, axis):
        for o in far(axis) + (0,):
            arrived(g, n, 1, rsib.at[m, g, o], o)
            arrived(g, n, 1, r_sib.at[m, g, o], o, scale_sems)
            part = ybuf[g, o] + value(rsib.at[m, g, o], r_sib.at[m, g, o])
            if o:
                j = back(axis, o)
                quantize(part, qring.at[m, g, o], s_ring.at[m, g, o])
                push(g, n, 0, qring.at[m, g, o], rring.at[m, g, j], o, j, device(axis, 0, o))
                push(g, n, 0, s_ring.at[m, g, o], r_ring.at[m, g, j], o, j, device(axis, 0, o), scale_sems)
            else:
                own[g] = part

    def scatter_end(g, m, n, axis):
        total = own[g]
        for o in near(axis):
            arrived(g, n, 0, rring.at[m, g, o], o)
            arrived(g, n, 0, r_ring.at[m, g, o], o, scale_sems)
            total = total + value(rring.at[m, g, o], r_ring.at[m, g, o])
        return total

    def product(g, m, come, go, scale, transposed):
        low, high = limits[0], limits[1]
        centre, half = 0.5 * (low + high), 0.5 * (high - low)
        rows = []
        for s in (0, 1):
            for o in range(NS):
                v = member(go, s, o)
                if come == "row":
                    slot = rem(div(v, NS) + xh, 2) * NS + rem(rem(v, NS) - z + NS, NS)
                else:
                    slot = rem(v + core, 2) * NS + rem(div(v, 2) + xl, 2) * 4 + rem(div(v, 4) - y + 4, 4)
                rows.append(unpack(ag[m, g, slot].astype(jnp.float32)) if G > 1 else ag[m, g, slot])
        x = jnp.concatenate(rows, axis=0).astype(jnp.bfloat16)
        kpart = jnp.dot(x, (kt if transposed else kd)[...], preferred_element_type=jnp.float32)
        mpart = jnp.dot(x, (mt if transposed else md)[...], preferred_element_type=jnp.float32)
        ybuf[g] = ((kpart - centre * mpart) * (scale / half)).reshape(2 * NS, ROWS, TILE)

    def held(m, g):
        return unpack(keep[m, g].astype(jnp.float32))

    def step(g, t):
        rows = slice(g * ROWS, (g + 1) * ROWS)
        if t == 0:
            gather_send(g, 0, 0, "row", keep.at[2, g])
        elif t == 1:
            gather_pass(g, 0, 0, "row")
        elif t == 2:
            gather_end(g, 0, 0, "row")
            product(g, 0, "row", "col", 1.0, True)
            scatter_send(g, 0, 1, "col")
        elif t == 3:
            scatter_pass(g, 0, 1, "col")
        elif t == 4:
            keep[0, g] = pack(scatter_end(g, 0, 1, "col")).astype(jnp.bfloat16)
            gather_send(g, 1, 2, "col", keep.at[0, g])
        elif t == 5:
            gather_pass(g, 1, 2, "col")
        elif t == 6:
            gather_end(g, 1, 2, "col")
            product(g, 1, "col", "row", 2.0, False)
            scatter_send(g, 1, 3, "row")
        elif t == 7:
            scatter_pass(g, 1, 3, "row")
        elif t == 8:
            keep[1, g] = pack(scatter_end(g, 1, 3, "row") - held(2, g)).astype(jnp.bfloat16)
            gather_send(g, 2, 4, "row", keep.at[1, g])
        elif t == 9:
            gather_pass(g, 2, 4, "row")
        elif t == 10:
            gather_end(g, 2, 4, "row")
            product(g, 2, "row", "col", 2.0, True)
            scatter_send(g, 2, 5, "col")
        elif t == 11:
            scatter_pass(g, 2, 5, "col")
        else:
            out[rows] = scatter_end(g, 2, 5, "col")
            first_out[rows] = held(0, g)

    for n, (g, t) in enumerate(ORDER):
        if n == 1:
            for load in (loads[1], loads[4], loads[5]):
                load.wait()
            build()
        step(g, t)
    for one in sent:
        one.wait_send()


def local(start, stiffness, mass, coords, lower, upper):
    slots = stiffness.shape[2]
    vmem, hbm = (pl.BlockSpec(memory_space=m) for m in (pltpu.VMEM, pl.ANY))
    half = (3, G, NS, PIECE, WIDE)
    scales = pltpu.VMEM((3, G, NS, 1, BLK), jnp.float32)
    sems = pltpu.SemaphoreType.DMA((G, 6, 2, NS))
    total, first = pl.pallas_call(
        kernel,
        out_shape=[pltpu.VMEM(start.shape, jnp.float32)] * 2,
        in_specs=[hbm] * 6,
        out_specs=[vmem] * 2,
        scratch_shapes=[
            pltpu.VMEM(start.shape, start.dtype),
            pltpu.VMEM((2, slots), jnp.int32),
            pltpu.VMEM((2, 1, 1), jnp.float32),
            pltpu.VMEM((BR * BR, BLK), jnp.int32),
            pltpu.SMEM((BR * BR, BLK), jnp.int32),
            pltpu.VMEM((slots, BLK, BLK), jnp.bfloat16),
            pltpu.VMEM((slots, BLK, BLK), jnp.bfloat16),
            pltpu.VMEM((TILE, TILE), jnp.bfloat16),
            pltpu.VMEM((TILE, TILE), jnp.bfloat16),
            pltpu.VMEM((TILE, TILE), jnp.bfloat16),
            pltpu.VMEM((TILE, TILE), jnp.bfloat16),
            pltpu.VMEM((G, 2 * NS, ROWS, TILE), jnp.float32),
            pltpu.VMEM((3, G, 2 * NS, PIECE, WIDE), jnp.bfloat16),
            pltpu.VMEM(half, jnp.int16),
            pltpu.VMEM(half, jnp.int16),
            pltpu.VMEM(half, jnp.int16),
            pltpu.VMEM(half, jnp.int16),
            pltpu.VMEM((G, ROWS, TILE), jnp.float32),
            pltpu.VMEM((3, G, PIECE, WIDE), jnp.bfloat16),
            scales, scales, scales, scales,
            pltpu.SemaphoreType.DMA((7,)),
            sems, sems, sems, sems,
        ],
        compiler_params=pltpu.CompilerParams(
            collective_id=0, has_side_effects=True, vmem_limit_bytes=57344 * 2**10
        ),
        name="filter",
    )(coords[0, 0].T, lower.reshape(1, 1), upper.reshape(1, 1), start,
      stiffness.reshape(stiffness.shape[2:]), mass.reshape(mass.shape[2:]))
    return total - first


def solution(mesh):
    placed = (
        P("row", "col"),
        P("row", "col", None, None, None),
        P("row", "col", None, None, None),
        P("row", "col", None, None),
        P(),
        P(),
    )
    return jax.shard_map(
        local, mesh=mesh, in_specs=placed, out_specs=P("col", "row"), check_vma=False
    )
```

```python
import jax
import jax.numpy as jnp
from jax import lax
from jax.experimental import pallas as pl
from jax.experimental.pallas import tpu as pltpu
from jax.sharding import PartitionSpec as P

MESH = pl.DeviceIdType.MESH
BLK = 128
BR = 8
TILE = 1024
PIECE = 16
G = 2
ROWS = PIECE // G
WIDE = TILE // G
ORDER = (
    (0, 0), (1, 0), (0, 1), (1, 1), (0, 2), (0, 3), (1, 2), (1, 3), (0, 4), (1, 4), (0, 5), (0, 6), (1, 5),
    (1, 6), (0, 7), (1, 7), (0, 8), (1, 8), (0, 9), (1, 9), (0, 10), (0, 11), (1, 10), (1, 11), (0, 12), (1, 12),
)
NS = 8
LATE = 5
TOP = 32766.0
TINY = 1e-33
ROW_NEAR = (1, 7, 2, 6, 3, 5, 4)
ROW_FAR = (4, 3, 5, 2, 6, 1, 7)
COL_NEAR = (4, 1, 3, 5, 7, 2, 6)
COL_FAR = (6, 2, 5, 7, 1, 3, 4)


def back(axis, o):
    return (-o) % NS if axis == "row" else (o // 4) * 4 + (-o) % 4


def rem(a, b):
    return lax.rem(a, jnp.int32(b))


def div(a, b):
    return lax.div(a, jnp.int32(b))


def flip(bit, s):
    return 1 - bit if s else bit


def kernel(pairs, lower, upper, start_hbm, khbm, mhbm, out, first_out, start, place, limits, inv_wide, inv, kslot, mslot, kt, mt, kd, md, ybuf, ag, qsib, rsib, qring, rring, own, keep,
           s_sib, s_ring, r_sib, r_ring, local_sem, send_sem, recv_sem, ssend_sem, srecv_sem):
    r = lax.axis_index("row")
    c = lax.axis_index("col")
    xh, z = div(r, NS), rem(r, NS)
    y, xl, core = div(c, 4), rem(div(c, 2), 2), rem(c, 2)

    def member(axis, s, o):
        if axis == "row":
            return flip(xh, s) * NS + rem(z + o, NS)
        return rem(y + o % 4, 4) * 4 + flip(xl, o // 4) * 2 + flip(core, s)

    def device(axis, s, o):
        m = member(axis, s, o)
        return (m, c) if axis == "row" else (r, m)

    barrier = pltpu.get_barrier_semaphore()
    for axis in ("row", "col"):
        for o in range(1, NS):
            pl.semaphore_signal(barrier, inc=1, device_id=device(axis, 0, o), device_id_type=MESH)
        pl.semaphore_signal(barrier, inc=1, device_id=device(axis, 1, 0), device_id_type=MESH)

    loads = [
        pltpu.make_async_copy(src, dst, local_sem.at[i])
        for i, (src, dst) in enumerate(
            ((start_hbm, start), (pairs, place), (khbm, kslot), (mhbm, mslot),
             (lower, limits.at[0]), (upper, limits.at[1]))
        )
    ]
    for load in loads:
        load.start()

    def pack(part):
        return part if G == 1 else jnp.concatenate([part[:, :WIDE], part[:, WIDE:]], axis=0)

    def unpack(piece):
        return piece if G == 1 else jnp.concatenate([piece[:ROWS], piece[ROWS:]], axis=1)

    loads[0].wait()
    for g in range(G):
        keep[2, g] = pack(start[...].astype(jnp.float32)[g * ROWS:(g + 1) * ROWS]).astype(jnp.bfloat16)

    def build():
        slots = place.shape[1]
        target = lax.broadcasted_iota(jnp.int32, (BR * BR, slots), 0)
        slot = lax.broadcasted_iota(jnp.int32, (BR * BR, slots), 1)
        found = (place[0:1] == target // BR) & (place[1:2] == target % BR)
        held_by = jnp.max(jnp.where(found, slot, -1), axis=1, keepdims=True)
        inv_wide[...] = jnp.broadcast_to(held_by, inv_wide.shape)
        index = pltpu.make_async_copy(inv_wide, inv, local_sem.at[6])
        index.start()
        index.wait()
        loads[2].wait()
        loads[3].wait()
        for t in range(BR * BR):
            s = inv[t, 0]
            live = s >= 0
            s = jnp.maximum(s, 0)
            zero = jnp.zeros((BLK, BLK), jnp.bfloat16)
            rows, cols = slice((t // BR) * BLK, (t // BR + 1) * BLK), slice((t % BR) * BLK, (t % BR + 1) * BLK)
            kblock = jnp.where(live, kslot[s], zero)
            mblock = jnp.where(live, mslot[s], zero)
            kd[rows, cols] = kblock
            md[rows, cols] = mblock
            kt[cols, rows] = kblock.T
            mt[cols, rows] = mblock.T

    pl.semaphore_wait(barrier, 2 * NS)

    sent = []

    def copy(g, n, side, src, dst, i, j, dev, sems=(send_sem, recv_sem)):
        return pltpu.make_async_remote_copy(
            src_ref=src, dst_ref=dst, send_sem=sems[0].at[g, n, side, i], recv_sem=sems[1].at[g, n, side, j],
            device_id=dev, device_id_type=MESH)

    def push(*args, **kw):
        one = copy(*args, **kw)
        one.start()
        sent.append(one)

    def arrived(g, n, side, dst, j, sems=(send_sem, recv_sem)):
        copy(g, n, side, dst, dst, 0, j, (r, c), sems).wait_recv()

    def near(axis):
        return ROW_NEAR if axis == "row" else COL_NEAR

    def far(axis):
        return ROW_FAR if axis == "row" else COL_FAR

    def gather_send(g, m, n, axis, src):
        buf = ag.at[m, g]
        push(g, n, 1, src, buf.at[NS], 0, 0, device(axis, 1, 0))
        for o in ROW_NEAR if axis == "row" else COL_FAR:
            j = back(axis, o)
            push(g, n, 0, src, buf.at[j], o, j, device(axis, 0, o))
        buf[0] = src[...]

    def gather_pass(g, m, n, axis):
        buf = ag.at[m, g]
        for o in near(axis):
            arrived(g, n, 0, buf.at[o], o)
            push(g, n, 1, buf.at[o], buf.at[NS + o], o, o, device(axis, 1, 0))

    def gather_end(g, m, n, axis):
        for o in (0,) + near(axis):
            arrived(g, n, 1, ag.at[m, g, NS + o], o)

    def quantize(part, q, sc):
        top = jnp.maximum(jnp.max(jnp.abs(part), keepdims=True), TINY)
        q[...] = jnp.round(pack(part * (TOP / top))).astype(jnp.int32).astype(jnp.int16)
        sc[...] = jnp.broadcast_to(top * (1.0 / TOP), (1, BLK))

    def value(q, sc):
        return unpack(q[...].astype(jnp.int32).astype(jnp.float32)) * sc[:, :1]

    scale_sems = (ssend_sem, srecv_sem)

    def scatter_send(g, m, n, axis):
        for o in far(axis) + (0,):
            quantize(ybuf[g, NS + o], qsib.at[m, g, o], s_sib.at[m, g, o])
            push(g, n, 1, qsib.at[m, g, o], rsib.at[m, g, o], o, o, device(axis, 1, 0))
            push(g, n, 1, s_sib.at[m, g, o], r_sib.at[m, g, o], o, o, device(axis, 1, 0), scale_sems)

    def scatter_pass(g, m, n, axis):
        for o in far(axis) + (0,):
            arrived(g, n, 1, rsib.at[m, g, o], o)
            arrived(g, n, 1, r_sib.at[m, g, o], o, scale_sems)
            part = ybuf[g, o] + value(rsib.at[m, g, o], r_sib.at[m, g, o])
            if o:
                j = back(axis, o)
                quantize(part, qring.at[m, g, o], s_ring.at[m, g, o])
                push(g, n, 0, qring.at[m, g, o], rring.at[m, g, j], o, j, device(axis, 0, o))
                push(g, n, 0, s_ring.at[m, g, o], r_ring.at[m, g, j], o, j, device(axis, 0, o), scale_sems)
            else:
                own[g] = part

    def scatter_end(g, m, n, axis):
        total = own[g]
        for o in near(axis):
            arrived(g, n, 0, rring.at[m, g, o], o)
            arrived(g, n, 0, r_ring.at[m, g, o], o, scale_sems)
            total = total + value(rring.at[m, g, o], r_ring.at[m, g, o])
        return total

    def product(g, m, come, go, scale, transposed):
        low, high = limits[0], limits[1]
        centre, half = 0.5 * (low + high), 0.5 * (high - low)
        rows = []
        for s in (0, 1):
            for o in range(NS):
                v = member(go, s, o)
                if come == "row":
                    slot = rem(div(v, NS) + xh, 2) * NS + rem(rem(v, NS) - z + NS, NS)
                else:
                    slot = rem(v + core, 2) * NS + rem(div(v, 2) + xl, 2) * 4 + rem(div(v, 4) - y + 4, 4)
                rows.append(unpack(ag[m, g, slot].astype(jnp.float32)) if G > 1 else ag[m, g, slot])
        x = jnp.concatenate(rows, axis=0).astype(jnp.bfloat16)
        kpart = jnp.dot(x, (kt if transposed else kd)[...], preferred_element_type=jnp.float32)
        mpart = jnp.dot(x, (mt if transposed else md)[...], preferred_element_type=jnp.float32)
        ybuf[g] = ((kpart - centre * mpart) * (scale / half)).reshape(2 * NS, ROWS, TILE)

    def held(m, g):
        return unpack(keep[m, g].astype(jnp.float32))

    def step(g, t):
        rows = slice(g * ROWS, (g + 1) * ROWS)
        if t == 0:
            gather_send(g, 0, 0, "row", keep.at[2, g])
        elif t == 1:
            gather_pass(g, 0, 0, "row")
        elif t == 2:
            gather_end(g, 0, 0, "row")
            product(g, 0, "row", "col", 1.0, True)
            scatter_send(g, 0, 1, "col")
        elif t == 3:
            scatter_pass(g, 0, 1, "col")
        elif t == 4:
            keep[0, g] = pack(scatter_end(g, 0, 1, "col")).astype(jnp.bfloat16)
            gather_send(g, 1, 2, "col", keep.at[0, g])
        elif t == 5:
            gather_pass(g, 1, 2, "col")
        elif t == 6:
            gather_end(g, 1, 2, "col")
            product(g, 1, "col", "row", 2.0, False)
            scatter_send(g, 1, 3, "row")
        elif t == 7:
            scatter_pass(g, 1, 3, "row")
        elif t == 8:
            keep[1, g] = pack(scatter_end(g, 1, 3, "row") - held(2, g)).astype(jnp.bfloat16)
            gather_send(g, 2, 4, "row", keep.at[1, g])
        elif t == 9:
            gather_pass(g, 2, 4, "row")
        elif t == 10:
            gather_end(g, 2, 4, "row")
            product(g, 2, "row", "col", 2.0, True)
            scatter_send(g, 2, 5, "col")
        elif t == 11:
            scatter_pass(g, 2, 5, "col")
        else:
            out[rows] = scatter_end(g, 2, 5, "col")
            first_out[rows] = held(0, g)

    marks = []
    for n, (g, t) in enumerate(ORDER):
        if n == 1:
            for load in (loads[1], loads[4], loads[5]):
                load.wait()
            build()
        step(g, t)
        marks.append(len(sent))
        if n >= LATE:
            for one in sent[marks[n - LATE - 1] if n > LATE else 0:marks[n - LATE]]:
                one.wait_send()
    for one in sent[marks[len(ORDER) - 1 - LATE]:]:
        one.wait_send()


def local(start, stiffness, mass, coords, lower, upper):
    slots = stiffness.shape[2]
    vmem, hbm = (pl.BlockSpec(memory_space=m) for m in (pltpu.VMEM, pl.ANY))
    half = (3, G, NS, PIECE, WIDE)
    scales = pltpu.VMEM((3, G, NS, 1, BLK), jnp.float32)
    sems = pltpu.SemaphoreType.DMA((G, 6, 2, NS))
    total, first = pl.pallas_call(
        kernel,
        out_shape=[pltpu.VMEM(start.shape, jnp.float32)] * 2,
        in_specs=[hbm] * 6,
        out_specs=[vmem] * 2,
        scratch_shapes=[
            pltpu.VMEM(start.shape, start.dtype),
            pltpu.VMEM((2, slots), jnp.int32),
            pltpu.VMEM((2, 1, 1), jnp.float32),
            pltpu.VMEM((BR * BR, BLK), jnp.int32),
            pltpu.SMEM((BR * BR, BLK), jnp.int32),
            pltpu.VMEM((slots, BLK, BLK), jnp.bfloat16),
            pltpu.VMEM((slots, BLK, BLK), jnp.bfloat16),
            pltpu.VMEM((TILE, TILE), jnp.bfloat16),
            pltpu.VMEM((TILE, TILE), jnp.bfloat16),
            pltpu.VMEM((TILE, TILE), jnp.bfloat16),
            pltpu.VMEM((TILE, TILE), jnp.bfloat16),
            pltpu.VMEM((G, 2 * NS, ROWS, TILE), jnp.float32),
            pltpu.VMEM((3, G, 2 * NS, PIECE, WIDE), jnp.bfloat16),
            pltpu.VMEM(half, jnp.int16),
            pltpu.VMEM(half, jnp.int16),
            pltpu.VMEM(half, jnp.int16),
            pltpu.VMEM(half, jnp.int16),
            pltpu.VMEM((G, ROWS, TILE), jnp.float32),
            pltpu.VMEM((3, G, PIECE, WIDE), jnp.bfloat16),
            scales, scales, scales, scales,
            pltpu.SemaphoreType.DMA((7,)),
            sems, sems, sems, sems,
        ],
        compiler_params=pltpu.CompilerParams(
            collective_id=0, has_side_effects=True, vmem_limit_bytes=57344 * 2**10
        ),
        name="filter",
    )(coords[0, 0].T, lower.reshape(1, 1), upper.reshape(1, 1), start,
      stiffness.reshape(stiffness.shape[2:]), mass.reshape(mass.shape[2:]))
    return total - first


def solution(mesh):
    placed = (
        P("row", "col"),
        P("row", "col", None, None, None),
        P("row", "col", None, None, None),
        P("row", "col", None, None),
        P(),
        P(),
    )
    return jax.shard_map(
        local, mesh=mesh, in_specs=placed, out_specs=P("col", "row"), check_vma=False
    )
```
